128 devices in a mesh: slab: 32 (over x, y, core), lane: 4 (over z).
Axes of the slice: x: 4, y: 4, z: 4, core: 2. Of those that a mesh axis runs over, the one named last changes fastest.
Arguments:
- particles: float32 [6, 262144], P(None, ('slab', 'lane')), as said below
- pair_list: int32 [32, 32768], P(None, ('slab', 'lane')), may hold values from 0 to 2303, as said below
- pair_count: int32 [32768], P(('slab', 'lane')), may hold values from 2 to 32, as said below
Outputs:
- short_forces: float32 [3, 262144], P(None, ('slab', 'lane'))
- long_forces: float32 [3, 262144], P(None, ('slab', 'lane'))
The draws below stay inside these ranges and needn't reach their ends.
Inputs may be any that keep to these rules, and one draw needn't show every extreme that they name: `particles`: column a*256+c of a device's block is atom a = 4*ax+2*ay+az of cluster c = (cx*4+cy)*16+cz; its position lies within 0.03 nm of lattice site ((2cx+ax+0.5)*0.3, (2cy+ay+0.5)*0.3, (2cz+az+0.5)*0.12*256/32) in the brick's own frame; charges lie in -1.5 to 1.5, row 4 in 0.003 to 0.01, row 5 in 3e-5 to 1e-4. `pair_list`: entry j = (3*(bx+1)+(by+1))*256+c' names cluster c' of the brick bx slab steps and by lane steps away (periodic); it lies within two cluster steps of the listing cluster along x and y and one along z (periodic in z); the entries of a column are distinct. Slots 0 to pair_count-1 of a cluster's column are used; loads differ widely between bricks.
All inputs are finite; a program needn't handle non-finite values.
Results may differ from the reference program's by a relative error of at most 0.0003.
Values sent between devices are 32-bit elements; how exact they have to be, the bound alone decides.
A program may use at most 192 MiB of HBM per device.

```python
import math
import jax
import jax.numpy as jnp
from jax import lax

LAT_X = 8
LAT_Y = 8
LZ_LAT = 32
CELLS_X = 15
CELLS_Y = 40
GZ = 256
JP = 32
ATOM_DEV = 2048
NCL = 256
ATOMS = 262144
CLUSTERS = 32768
GX = 480
GY = 160
N_SLAB = 32
N_LANE = 4


def lattice_sites():
    global_index = jnp.arange(ATOMS, dtype=jnp.int32)
    local_index = global_index % ATOM_DEV
    atom_slot = local_index // NCL
    cluster = local_index % NCL
    per_y = LAT_Y // 2
    per_z = LZ_LAT // 2
    cluster_x = cluster // (per_y * per_z)
    cluster_y = cluster // per_z % per_y
    cluster_z = cluster % per_z
    site_x = 2 * cluster_x + atom_slot // 4
    site_y = 2 * cluster_y + atom_slot // 2 % 2
    site_z = 2 * cluster_z + atom_slot % 2
    return (site_x, site_y, site_z)


def draw_particles(key, part):
    key = jax.random.fold_in(key, 7)
    keys = jax.random.split(key, 4)
    site_x, site_y, site_z = lattice_sites()
    step_z = GZ * 0.12 / LZ_LAT
    jitter = 0.012 * jax.random.truncated_normal(keys[0], -2.5, 2.5, (3, ATOMS), jnp.float32)
    pos_x = (site_x.astype(jnp.float32) + 0.5) * 0.3 + jitter[0]
    pos_y = (site_y.astype(jnp.float32) + 0.5) * 0.3 + jitter[1]
    pos_z = (site_z.astype(jnp.float32) + 0.5) * step_z + jitter[2]
    layer_sign = (1 - 2 * (site_y % 2)).astype(jnp.float32)
    magnitude = 1.1 + 0.4 * jax.random.truncated_normal(keys[1], -1.0, 1.0, (ATOMS,), jnp.float32)
    charge = layer_sign * magnitude
    six_root = jnp.exp(jax.random.uniform(keys[2], (ATOMS,), jnp.float32, math.log(0.003), math.log(0.01)))
    twelve_root = jnp.exp(jax.random.uniform(keys[3], (ATOMS,), jnp.float32, math.log(3e-05), math.log(0.0001)))
    return jnp.stack([pos_x, pos_y, pos_z, charge, six_root, twelve_root])


def draw_pair_list(key, part):
    key = jax.random.fold_in(key, 11)
    per_x = LAT_X // 2
    per_y = LAT_Y // 2
    per_z = LZ_LAT // 2
    cluster = jnp.arange(CLUSTERS, dtype=jnp.int32) % NCL
    cluster_x = cluster // (per_y * per_z)
    cluster_y = cluster // per_z % per_y
    cluster_z = cluster % per_z
    neighbor_id = jnp.arange(75, dtype=jnp.int32)
    move_x = neighbor_id // 15 - 2
    move_y = neighbor_id // 3 % 5 - 2
    move_z = neighbor_id % 3 - 1
    scores = jax.random.randint(key, (CLUSTERS, 75), 0, 1 << 20) * 75 + neighbor_id[None, :]
    picked = jnp.argsort(scores, axis=1)[:, :JP]
    target_x = cluster_x[:, None] + move_x[picked]
    target_y = cluster_y[:, None] + move_y[picked]
    target_z = (cluster_z[:, None] + move_z[picked]) % per_z
    brick_step_x = jnp.floor_divide(target_x, per_x)
    brick_step_y = jnp.floor_divide(target_y, per_y)
    inner_x = target_x - brick_step_x * per_x
    inner_y = target_y - brick_step_y * per_y
    slot_value = ((brick_step_x + 1) * 3 + brick_step_y + 1) * NCL + (inner_x * per_y + inner_y) * per_z + target_z
    return slot_value.T.astype(jnp.int32)


def draw_pair_count(key, part):
    key = jax.random.fold_in(key, 13)
    keys = jax.random.split(key, 2)
    devices = N_SLAB * N_LANE
    brick_fill = jax.random.randint(keys[0], (devices,), JP // 8, JP + 1)
    fill_of = jnp.repeat(brick_fill, NCL)
    spread_draw = jax.random.randint(keys[1], (CLUSTERS,), 0, 1 << 20)
    counts = fill_of - spread_draw % (fill_of // 2 + 1)
    counts = counts.at[0].set(JP).at[1].set(JP // 16)
    return counts.astype(jnp.int32)


def setup_inputs(seed: int = 0) -> dict:
    arg_keys = jax.random.split(jax.random.key(seed), 4)
    particles = draw_particles(jax.random.fold_in(arg_keys[3], 71), 0)
    pair_list = draw_pair_list(jax.random.fold_in(arg_keys[3], 71), 0)
    pair_count = draw_pair_count(jax.random.fold_in(arg_keys[3], 71), 0)
    return {"particles": particles, "pair_list": pair_list, "pair_count": pair_count}


SPACING = 0.3
CELL_Z = 0.12
CUTOFF = 1.2
EWALD_BETA = 2.6
slot_block = 16

def spline_value(argument):
    magnitude = jnp.abs(argument)
    inner = 2.0 / 3.0 - magnitude * magnitude + 0.5 * magnitude * magnitude * magnitude
    outer = jnp.maximum(2.0 - magnitude, 0.0) ** 3 / 6.0
    return jnp.where(magnitude < 1.0, inner, outer)

def spline_slope(argument):
    magnitude = jnp.abs(argument)
    inner = argument * (1.5 * magnitude - 2.0)
    outer = -jnp.sign(argument) * 0.5 * jnp.maximum(2.0 - magnitude, 0.0) ** 2
    return jnp.where(magnitude < 1.0, inner, outer)

def stencil(coordinate):
    lowest = jnp.floor(coordinate) - 1.0
    cell_pos = lowest[None, :] + jnp.arange(4).astype(coordinate.dtype)[:, None]
    offset = coordinate[None, :] - cell_pos
    return (cell_pos.astype(jnp.int32), spline_value(offset), spline_slope(offset))

def signed_wave(wave_index, length_count):
    return jnp.where(wave_index < (length_count + 1) // 2, wave_index, wave_index - length_count)

def spline_modulus(wave_index, length_count):
    angle = wave_index.astype(jnp.float32) * (2.0 * math.pi / length_count)
    return 1.0 / (2.0 / 3.0 + jnp.cos(angle) / 3.0) ** 2

def influence(wave_x, wave_y, wave_z, count_x, count_y, length_x, length_y):
    length_z = GZ * CELL_Z
    freq_x = signed_wave(wave_x, count_x).astype(jnp.float32) / length_x
    freq_y = signed_wave(wave_y, count_y).astype(jnp.float32) / length_y
    freq_z = signed_wave(wave_z, GZ).astype(jnp.float32) / length_z
    norm_sq = freq_x * freq_x + freq_y * freq_y + freq_z * freq_z
    safe_sq = jnp.where(norm_sq > 0, norm_sq, 1.0)
    moduli = spline_modulus(wave_x, count_x) * spline_modulus(wave_y, count_y) * spline_modulus(wave_z, GZ)
    value = jnp.exp(-(math.pi / EWALD_BETA) ** 2 * safe_sq) * moduli / (math.pi * length_x * length_y * length_z * safe_sq)
    return jnp.where(norm_sq > 0, value, 0.0)

def pair_terms(owned, nearby, slot_rows, live_mask, center):
    joined = jnp.take(nearby, slot_rows, axis=2)
    own_side = owned[:, None, None, :, :]
    far_side = joined[:, :, :, None, :]
    diff_x = own_side[0] - far_side[0]
    diff_y = own_side[1] - far_side[1]
    diff_z = own_side[2] - far_side[2]
    box_z = GZ * CELL_Z
    diff_z = diff_z - box_z * jnp.floor(diff_z / box_z + 0.5)
    atom_ids = jnp.arange(8)
    same_atom = (slot_rows == center[None, :])[None, :, None, :] & (atom_ids[:, None] == atom_ids[None, :])[:, None, :, None]
    keep = live_mask[None, :, None, :] & jnp.logical_not(same_atom)
    dist_sq = diff_x * diff_x + diff_y * diff_y + diff_z * diff_z
    safe_sq = jnp.where(keep, dist_sq, 1.0)
    inverse = 1.0 / safe_sq
    distance = jnp.sqrt(safe_sq)
    inverse_six = inverse * inverse * inverse
    dispersion = (12.0 * own_side[5] * far_side[5] * inverse_six - 6.0 * own_side[4] * far_side[4]) * inverse_six
    coulomb = own_side[3] * far_side[3] * (jax.scipy.special.erfc(EWALD_BETA * distance) / distance + 2.0 * EWALD_BETA / math.sqrt(math.pi) * jnp.exp(-EWALD_BETA ** 2 * safe_sq))
    switch = jnp.maximum(1.0 - safe_sq / (CUTOFF * CUTOFF), 0.0) ** 2
    scalar = jnp.where(keep, (dispersion + coulomb) * inverse * switch, 0.0)
    return jnp.stack([lax.optimization_barrier(jnp.sum(scalar * diff_x, axis=(0, 1))), lax.optimization_barrier(jnp.sum(scalar * diff_y, axis=(0, 1))), lax.optimization_barrier(jnp.sum(scalar * diff_z, axis=(0, 1)))])

def short_range(owned, nearby, pairs_dev, counts_dev):
    clusters = owned.shape[2]
    center = 4 * clusters + jnp.arange(clusters, dtype=jnp.int32)

    def block_step(block_id, running):
        first_slot = (block_id * slot_block).astype(jnp.int32)
        slot_rows = lax.dynamic_slice_in_dim(pairs_dev, first_slot, slot_block, 0)
        live_mask = (first_slot + jnp.arange(slot_block, dtype=jnp.int32))[:, None] < counts_dev[None, :]
        return running + pair_terms(owned, nearby, slot_rows, live_mask, center)
    return lax.fori_loop(0, JP // slot_block, block_step, jnp.zeros((3, 8, clusters), owned.dtype))

def reference(particles, pair_list, pair_count):
    brick_x = LAT_X * SPACING
    brick_y = LAT_Y * SPACING
    devices = N_SLAB * N_LANE
    bricks = particles.reshape(6, N_SLAB, N_LANE, ATOM_DEV)
    stacked = []
    for step_x in (-1, 0, 1):
        for step_y in (-1, 0, 1):
            rolled = jnp.roll(bricks, (-step_x, -step_y), axis=(1, 2))
            rolled = jnp.concatenate([rolled[0:1] + step_x * brick_x, rolled[1:2] + step_y * brick_y, rolled[2:]], axis=0)
            stacked.append(rolled.reshape(6, devices, ATOM_DEV))
    placed = jnp.stack(stacked)

    def one_device(device):
        nearby = lax.dynamic_index_in_dim(placed, device, 2, keepdims=False)
        owned = nearby[4].reshape(6, 8, NCL)
        nearby = nearby.reshape(9, 6, 8, NCL).transpose(1, 2, 0, 3).reshape(6, 8, 9 * NCL)
        pairs_dev = lax.dynamic_slice_in_dim(pair_list, device * NCL, NCL, 1)
        counts_dev = lax.dynamic_slice_in_dim(pair_count, device * NCL, NCL, 0)
        return short_range(owned, nearby, pairs_dev, counts_dev).reshape(3, ATOM_DEV)
    short_all = lax.map(one_device, jnp.arange(devices, dtype=jnp.int32))
    short_forces = short_all.transpose(1, 0, 2).reshape(3, ATOMS)
    device_of = jnp.arange(ATOMS, dtype=jnp.int32) // ATOM_DEV
    slab_pos = (device_of // N_LANE).astype(particles.dtype)
    lane_pos = (device_of % N_LANE).astype(particles.dtype)
    cell_x = brick_x / CELLS_X
    cell_y = brick_y / CELLS_Y
    frac_x = (particles[0] + slab_pos * brick_x) / cell_x
    frac_y = (particles[1] + lane_pos * brick_y) / cell_y
    frac_z = particles[2] / CELL_Z
    charge = particles[3]
    pieces = 8
    piece_size = ATOMS // pieces
    flat_grid = jnp.zeros(GX * GY * GZ, particles.dtype)
    stencils = []
    for piece_id in range(pieces):
        lower = piece_id * piece_size
        upper = lower + piece_size
        index_x, weight_x, slope_x = stencil(frac_x[lower:upper])
        index_y, weight_y, slope_y = stencil(frac_y[lower:upper])
        index_z, weight_z, slope_z = stencil(frac_z[lower:upper])
        flat_index = ((index_x % GX)[:, None, None, :] * GY + (index_y % GY)[None, :, None, :]) * GZ + (index_z % GZ)[None, None, :, :]
        weights = charge[lower:upper] * weight_x[:, None, None, :] * weight_y[None, :, None, :] * weight_z[None, None, :, :]
        flat_grid = flat_grid.at[flat_index.reshape(-1)].add(weights.reshape(-1))
        stencils.append((flat_index, weight_x, weight_y, weight_z, slope_x, slope_y, slope_z))
    charge_grid = flat_grid.reshape(GX, GY, GZ)
    kernel = influence(jnp.arange(GX)[:, None, None], jnp.arange(GY)[None, :, None], jnp.arange(GZ)[None, None, :], GX, GY, brick_x * N_SLAB, brick_y * N_LANE)
    spectrum = jnp.fft.fftn(charge_grid)
    potential = jnp.real(jnp.fft.ifftn(spectrum * kernel)) * (GX * GY * GZ)
    flat_potential = potential.reshape(-1)
    long_parts = []
    for piece_id in range(pieces):
        lower = piece_id * piece_size
        upper = lower + piece_size
        flat_index, weight_x, weight_y, weight_z, slope_x, slope_y, slope_z = stencils[piece_id]
        sampled = flat_potential[flat_index]
        along_x = lax.optimization_barrier(jnp.sum(sampled * (slope_x / cell_x)[:, None, None, :] * weight_y[None, :, None, :] * weight_z[None, None, :, :], axis=(0, 1, 2)))
        along_y = lax.optimization_barrier(jnp.sum(sampled * weight_x[:, None, None, :] * (slope_y / cell_y)[None, :, None, :] * weight_z[None, None, :, :], axis=(0, 1, 2)))
        along_z = lax.optimization_barrier(jnp.sum(sampled * weight_x[:, None, None, :] * weight_y[None, :, None, :] * (slope_z / CELL_Z)[None, None, :, :], axis=(0, 1, 2)))
        long_parts.append(-charge[lower:upper] * jnp.stack([along_x, along_y, along_z]))
    long_forces = jnp.concatenate(long_parts, axis=1)
    return (short_forces, long_forces)
```

```python
import functools
import math

import jax
import jax.numpy as jnp
import numpy as np
from jax import lax
from jax.experimental import pallas as pl
from jax.experimental.pallas import tpu as pltpu
from jax.sharding import PartitionSpec as P

SPACING = 0.3
CELL_Z = 0.12
CUTOFF = 1.2
EWALD_BETA = 2.6
CELLS_X = 15
CELLS_Y = 40
GZ = 256
N_SLAB = 32
N_LANE = 4
GX = CELLS_X * N_SLAB
GY = CELLS_Y * N_LANE
BRICK = 8 * SPACING
HX = BRICK / CELLS_X
HY = BRICK / CELLS_Y
BOX_Z = GZ * CELL_Z
SITE_Z = BOX_Z / 32
DEVICES = N_SLAB * N_LANE
WIN_X = 18
ERFCX = (
    0.2256758607181025,
    0.22566977328080512,
    0.2078385838830704,
    0.1685781716404984,
    0.1412773409832938,
    -0.005255409952977477,
    0.1686438579877198,
    -0.18261534673649704,
    0.050187288302216415,
)
f32 = jnp.float32
VMEM = pl.BlockSpec(memory_space=pltpu.VMEM)


def x_window(site):
    low = 1.875 * (site + 0.5) - 0.1875
    high = 1.875 * (site + 0.5) + 0.1875
    first = math.floor(low) - 1
    last = math.ceil(high) + 1
    return [cell for cell in range(first, last + 1) if cell - 2 < high - 1e-6 and cell + 2 > low + 1e-6]


X_WINDOWS = [x_window(site) for site in range(8)]


def dft_basis(count):
    half = count // 2
    waves = np.concatenate([np.arange(half + 1), np.arange(1, half)])
    is_sine = np.arange(count) > half
    phase = np.outer(waves, np.arange(count)) % count
    angle = phase * (2.0 * np.pi / count)
    return waves, np.where(is_sine[:, None], np.sin(angle), np.cos(angle))


def wave_factor(waves, count, length):
    freq_sq = (waves / length) ** 2
    modulus = (2.0 / 3.0 + np.cos(2.0 * np.pi * waves / count) / 3.0) ** -2
    twice = np.where((waves == 0) | (2 * waves == count), 1.0, 2.0)
    return np.exp(-((np.pi / EWALD_BETA) ** 2) * freq_sq) * modulus * twice, freq_sq


def tables():
    waves_x, basis_x = dft_basis(GX)
    waves_y, basis_y = dft_basis(GY)
    cells = (15 * np.arange(N_SLAB)[None, :] + np.arange(WIN_X)[:, None] - 1) % GX
    forward_x = basis_x[:, cells.reshape(-1)]
    lane, cy, jy, ay = np.meshgrid(np.arange(4), np.arange(4), np.arange(4), np.arange(2), indexing="ij")
    rows = 40 * lane + 5 * (2 * cy + ay) + jy + 1
    forward_y = basis_y[:, rows.reshape(-1)].T
    kz = np.concatenate([np.arange(128), [128], np.arange(1, 128)])
    sine = np.arange(256) > 128
    jz, az, cy, cz = np.meshgrid(np.arange(5), np.arange(2), np.arange(4), np.arange(16), indexing="ij")
    cell = (8 * (2 * cz + az) + jz + 2).reshape(-1)
    angle = (np.outer(kz, cell) % GZ) * (2.0 * np.pi / GZ)
    basis_z = np.where(sine[:, None], np.sin(angle), np.cos(angle))
    gain_x, sq_x = wave_factor(waves_x, GX, BRICK * N_SLAB)
    gain_y, sq_y = wave_factor(waves_y, GY, BRICK * N_LANE)
    gain_z, sq_z = wave_factor(kz, GZ, BOX_Z)
    gain_z = gain_z / (np.pi * BRICK * N_SLAB * BRICK * N_LANE * BOX_Z)
    column = np.stack([gain_x, sq_x], axis=1)
    row = np.stack([gain_y, sq_y])
    plane = np.stack([gain_z.reshape(2, 128), sq_z.reshape(2, 128)], axis=-1).transpose(1, 0, 2)
    return {
        "z": basis_z.astype(np.float32),
        "x": forward_x.astype(np.float32),
        "xt": np.ascontiguousarray(forward_x.T).astype(np.float32),
        "y": forward_y.astype(np.float32),
        "yt": np.ascontiguousarray(forward_y.T).astype(np.float32),
        "col": column.astype(np.float32),
        "row": row.astype(np.float32),
        "plane": plane.astype(np.float32),
    }


def lanes(shape=(8, 128)):
    return lax.broadcasted_iota(jnp.int32, shape, 1)


def sublanes(shape=(8, 128)):
    return lax.broadcasted_iota(jnp.int32, shape, 0)


def ahead(value, step):
    return pltpu.roll(value, (-step) % 128, axis=1)


def matmul(left, right, transposed=False):
    dims = (((1,), (1,)), ((), ())) if transposed else (((1,), (0,)), ((), ()))
    return lax.dot_general(
        left, right, dims, precision=lax.Precision.HIGHEST, preferred_element_type=f32
    )


def spline(offset, slope):
    size = jnp.abs(offset)
    outer = jnp.maximum(2.0 - size, 0.0)
    outer_sq = outer * outer
    near = size < 1.0
    value = jnp.where(near, 2.0 / 3.0 + size * size * (0.5 * size - 1.0), outer_sq * outer * (1.0 / 6.0))
    if not slope:
        return value
    half = 0.5 * outer_sq
    derivative = jnp.where(near, offset * (1.5 * size - 2.0), jnp.where(offset < 0.0, half, -half))
    return value, derivative


def pick_site(z_ref, site, attr):
    even = jnp.broadcast_to(z_ref[0, site, attr : attr + 1, :], (8, 128))
    odd = jnp.broadcast_to(z_ref[1, site, attr : attr + 1, :], (8, 128))
    return jnp.where(sublanes() % 2 == 0, even, odd)


def site_offsets(z_ref, site):
    lane = lanes()
    sub = sublanes()
    along_x = (pick_site(z_ref, site, 0) - (site + 0.5) * SPACING) * (1.0 / HX)
    site_y = (2 * ((lane >> 4) & 3) + (sub & 1)).astype(f32)
    along_y = (pick_site(z_ref, site, 1) - (site_y + 0.5) * SPACING) * (1.0 / HY)
    site_z = (2 * (lane & 15) + (lane >> 6)).astype(f32)
    along_z = (pick_site(z_ref, site, 2) - (site_z + 0.5) * SITE_Z) * (1.0 / CELL_Z)
    along_y = along_y + (1.5 - (sub >> 1).astype(f32))
    return along_x, along_y, along_z, pick_site(z_ref, site, 3)


def pack_particles(part_ref, z_ref):
    lane = lanes((6, 128))
    low = lane < 64
    for ax in range(2):
        for ay in range(2):
            for pair in range(2):
                first = ((ax * 2 + ay) * 2) * 256 + pair * 128
                v0 = part_ref[:, first : first + 128]
                v1 = part_ref[:, first + 256 : first + 384]
                x = 4 * pair + ax
                z_ref[ay, x, 0:6, :] = jnp.where(low, v0, ahead(v1, 64))
                z_ref[ay, x + 2, 0:6, :] = jnp.where(low, ahead(v0, 64), v1)
    for x in range(8):
        even = z_ref[0, x, 0:6, :]
        odd = z_ref[1, x, 0:6, :]
        upper = ((lane >> 5) & 1) == 1
        z_ref[2, x, 0:6, :] = jnp.where(upper, even, ahead(odd, 32))
        z_ref[3, x, 0:6, :] = jnp.where(upper, ahead(odd, -32), even)


def unpack_forces(o_ref, out_ref):
    low = lanes() < 64
    for ax in range(2):
        for ay in range(2):
            for pair in range(2):
                first = ((ax * 2 + ay) * 2) * 256 + pair * 128
                x = 4 * pair + ax
                even = o_ref[ay, x]
                odd = o_ref[ay, x + 2]
                out_ref[:, first : first + 128] = jnp.where(low, even, ahead(odd, 64))[0:3]
                out_ref[:, first + 256 : first + 384] = jnp.where(low, ahead(even, 64), odd)[0:3]


def spread_charges(z_ref, ball_ref):
    lane_cy = (lanes() >> 4) & 3
    grid = {}

    def flush(cell):
        column = cell + 1
        for jz in range(5):
            value = grid.pop((cell, jz))
            for cy in range(4):
                row = (column * 4 + cy) * 8
                ball_ref[row : row + 8, jz * 128 : (jz + 1) * 128] = jnp.where(lane_cy == cy, value, 0.0)

    for site in range(8):
        along_x, along_y, along_z, charge = site_offsets(z_ref, site)
        charge_y = charge * spline(along_y, False)
        charge_yz = [charge_y * spline(along_z + (2.0 - jz), False) for jz in range(5)]
        for cell in X_WINDOWS[site]:
            weight = spline(along_x + (1.875 * (site + 0.5) - cell), False)
            for jz in range(5):
                term = weight * charge_yz[jz]
                key = (cell, jz)
                grid[key] = grid[key] + term if key in grid else term
        coming = X_WINDOWS[site + 1][0] if site < 7 else 99
        for cell in sorted({key[0] for key in grid}):
            if cell < coming:
                flush(cell)


def spread_kernel(part_ref, table_ref, z_ref, send_ref, ball_ref):
    z_ref[...] = jnp.zeros_like(z_ref)
    pack_particles(part_ref, z_ref)
    spread_charges(z_ref, ball_ref)
    table = table_ref[...]
    for tile in range(5):
        rows = 128 if tile < 4 else 64
        result = matmul(table, ball_ref[tile * 128 : tile * 128 + rows, :], True)
        if rows < 128:
            result = jnp.concatenate([result, jnp.zeros((256, 128 - rows), f32)], axis=1)
        send_ref[:, tile, :] = result[0:128]
        send_ref[:, 5 + tile, :] = result[128:256]


def swap_quarters(parts):
    half = (lanes(parts[0].shape) >> 6) == 0
    quarter = ((lanes(parts[0].shape) >> 5) & 1) == 0
    a0 = jnp.where(half, parts[0], ahead(parts[2], 64))
    a2 = jnp.where(half, ahead(parts[0], 64), parts[2])
    a1 = jnp.where(half, parts[1], ahead(parts[3], 64))
    a3 = jnp.where(half, ahead(parts[1], 64), parts[3])
    b0 = jnp.where(quarter, a0, ahead(a1, -32))
    b1 = jnp.where(quarter, ahead(a0, 32), a1)
    b2 = jnp.where(quarter, a2, ahead(a3, -32))
    b3 = jnp.where(quarter, ahead(a2, 32), a3)
    return [b0, b1, b2, b3]


def middle_kernel(recv_ref, x_ref, xt_ref, y_ref, yt_ref, col_ref, row_ref, plane_ref, send_ref, both_ref):
    me = lax.axis_index("lane") * N_SLAB + lax.axis_index("slab")
    for half in range(2):
        for tile in range(5):
            parts = [recv_ref[lane * 32 : (lane + 1) * 32, half * 5 + tile, :] for lane in range(4)]
            swapped = swap_quarters(parts)
            for m in range(4):
                cell = 4 * tile + m
                if cell < WIN_X:
                    both_ref[cell * 32 : (cell + 1) * 32, half * 128 : (half + 1) * 128] = swapped[m]
    waves_x = matmul(x_ref[...], both_ref[...])
    back = []
    mine = plane_ref[pl.ds(me, 1)]
    for half in range(2):
        plane = matmul(waves_x[:, half * 128 : (half + 1) * 128], y_ref[...])
        sum_sq = col_ref[:, 1:2] + row_ref[1:2, :] + mine[0, half : half + 1, 1:2]
        gain = (col_ref[:, 0:1] * mine[0, half : half + 1, 0:1]) * row_ref[0:1, :]
        gain = jnp.where(sum_sq > 0.0, gain / jnp.where(sum_sq > 0.0, sum_sq, 1.0), 0.0)
        back.append(matmul(plane * gain, yt_ref[...]))
    both_ref[...] = matmul(xt_ref[...], jnp.concatenate(back, axis=1))
    for half in range(2):
        for tile in range(5):
            parts = []
            for m in range(4):
                cell = min(4 * tile + m, WIN_X - 1)
                parts.append(both_ref[cell * 32 : (cell + 1) * 32, half * 128 : (half + 1) * 128])
            swapped = swap_quarters(parts)
            for lane in range(4):
                send_ref[lane * 32 : (lane + 1) * 32, half * 5 + tile, :] = swapped[lane]


def interpolate(z_ref, pot_ref, o_ref):
    lane_cy = (lanes() >> 4) & 3
    sub = sublanes()

    def potential(cell, jz):
        row = (cell + 1) * 32
        value = pot_ref[row : row + 8, jz * 128 : (jz + 1) * 128]
        for cy in range(1, 4):
            other = pot_ref[row + 8 * cy : row + 8 * cy + 8, jz * 128 : (jz + 1) * 128]
            value = jnp.where(lane_cy == cy, other, value)
        return value

    held = {}
    for site in range(8):
        along_x, along_y, along_z, charge = site_offsets(z_ref, site)
        value_y, slope_y = spline(along_y, True)
        plain = [None] * 5
        sloped = [None] * 5
        for cell in X_WINDOWS[site]:
            value_x, slope_x = spline(along_x + (1.875 * (site + 0.5) - cell), True)
            for jz in range(5):
                key = (cell, jz)
                if key not in held:
                    held[key] = potential(cell, jz)
                sample = held[key]
                first = value_x * sample
                second = slope_x * sample
                plain[jz] = first if plain[jz] is None else plain[jz] + first
                sloped[jz] = second if sloped[jz] is None else sloped[jz] + second
        coming = X_WINDOWS[site + 1][0] if site < 7 else 99
        for key in [key for key in held if key[0] < coming]:
            del held[key]
        along = [None] * 3
        for jz in range(5):
            value_z, slope_z = spline(along_z + (2.0 - jz), True)
            terms = (sloped[jz] * value_z, plain[jz] * value_z, plain[jz] * slope_z)
            for axis in range(3):
                along[axis] = terms[axis] if along[axis] is None else along[axis] + terms[axis]
        scale = (
            value_y * charge * (-1.0 / HX),
            slope_y * charge * (-1.0 / HY),
            value_y * charge * (-1.0 / CELL_Z),
        )
        for axis in range(3):
            force = along[axis] * scale[axis]
            force = force + pltpu.roll(force, 4, axis=0)
            force = force + pltpu.roll(force, 2, axis=0)
            o_ref[0, site, axis : axis + 1, :] = force[0:1]
            o_ref[1, site, axis : axis + 1, :] = force[1:2]


def force_kernel(recv_ref, z_ref, table_ref, out_ref, pot_ref, o_ref):
    table = table_ref[...]
    for tile in range(5):
        rows = 128 if tile < 4 else 64
        left = jnp.concatenate([recv_ref[:, tile, :].T, recv_ref[:, 5 + tile, :].T], axis=1)
        pot_ref[tile * 128 : tile * 128 + rows, :] = matmul(left[0:rows], table)
    interpolate(z_ref, pot_ref, o_ref)
    unpack_forces(o_ref, out_ref)


def site_steps():
    steps = []
    for ez in (0, 1, -1):
        for ex in range(-5, 6):
            for ey in range(-5, 6):
                if ex == 0 and ey == 0 and ez == 0:
                    continue
                reach = 0.0
                for step, pitch in ((ex, SPACING), (ey, SPACING), (ez, SITE_Z)):
                    reach += max(abs(step) * pitch - 0.0601, 0.0) ** 2
                if reach < CUTOFF * CUTOFF:
                    steps.append((ex, ey, ez))
    return steps


STEPS = site_steps()
Y_RANGE = {0: range(-4, 6), 1: range(-2, 4), -1: range(-2, 4)}
SLOTS = {}
for _ez in (0, 1, -1):
    for _y in Y_RANGE[_ez]:
        SLOTS[(_y, _ez)] = len(SLOTS)


def near_kernel(center_ref, low_ref, high_ref, list_ref, count_ref, out_ref, ext_ref, o_ref):
    lane = lanes((16, 128))
    lane_cy = (lane >> 4) & 3
    lane_cz = lane & 15
    lane_az = lane >> 6
    x_row = sublanes((16, 128))
    shift_x = jnp.where(x_row < 4, -BRICK, jnp.where(x_row >= 12, BRICK, 0.0))

    for attr in range(6):
        own = [center_ref[parity, :, attr, :] for parity in range(2)]
        low = low_ref[:, attr, :]
        high = high_ref[:, attr, :]
        if attr == 0:
            own = [value + shift_x for value in own]
            low = low + shift_x
            high = high + shift_x
        if attr == 1:
            low = low - BRICK
            high = high + BRICK
        for y in Y_RANGE[0]:
            parity, step = y % 2, y // 2
            value = own[parity]
            if step > 0:
                value = jnp.where(
                    lane_cy + step >= 4, ahead(high, 16 * (step - 4 + 2 * parity)), ahead(value, 16 * step)
                )
            if step < 0:
                value = jnp.where(
                    lane_cy + step < 0, ahead(low, 16 * (step + 4 - 2 * parity)), ahead(value, 16 * step)
                )
            ext_ref[SLOTS[(y, 0)], attr] = value
            if y in Y_RANGE[1]:
                flipped = ahead(value, 64)
                up = jnp.where(lane_cz == 15, ahead(value, 49), ahead(value, 65))
                down = jnp.where(lane_cz == 0, ahead(value, 79), ahead(value, 63))
                if attr == 2:
                    up = jnp.where(lane_cz == 15, up + BOX_Z, up)
                    down = jnp.where(lane_cz == 0, down - BOX_Z, down)
                ext_ref[SLOTS[(y, 1)], attr] = jnp.where(lane_az == 0, flipped, up)
                ext_ref[SLOTS[(y, -1)], attr] = jnp.where(lane_az == 1, flipped, down)

    column = lax.broadcasted_iota(jnp.int32, (32, 256), 1)
    slot = lax.broadcasted_iota(jnp.int32, (32, 256), 0)
    entry = list_ref[...]
    brick = entry >> 8
    brick_x = jnp.where(brick >= 6, 2, jnp.where(brick >= 3, 1, 0))
    brick_y = brick - 3 * brick_x
    step_x = 4 * (brick_x - 1) + ((entry >> 6) & 3) - (column >> 6)
    step_y = 4 * (brick_y - 1) + ((entry >> 4) & 3) - ((column >> 4) & 3)
    step_z = ((entry & 15) - (column & 15)) & 15
    bit = jnp.left_shift(jnp.int32(1), 5 * (step_x + 2) + step_y + 2)
    bit = jnp.where(slot < count_ref[...], bit, 0)
    lane8 = lanes()
    row8 = sublanes()
    words = []
    for z_code in (0, 1, 15):
        chosen = jnp.where(step_z == z_code, bit, 0)
        total = chosen[0:8] + chosen[8:16] + chosen[16:24] + chosen[24:32]
        for turn in (4, 2, 1):
            total = total + pltpu.roll(total, turn, axis=0)
        word = None
        for pair in range(2):
            part = total[:, pair * 128 : (pair + 1) * 128]
            flipped = ahead(part, 64)
            even = jnp.where(lane8 < 64, part, flipped)
            odd = jnp.where(lane8 < 64, flipped, part)
            if word is None:
                word = jnp.where(row8 < 2, even, odd)
            else:
                word = jnp.where(row8 < 4, word, jnp.where(row8 < 6, even, odd))
        words.append(word)
    az8 = lane8 >> 6
    by_z = {
        0: words[0],
        1: jnp.where(az8 == 1, words[1], words[0]),
        -1: jnp.where(az8 == 0, words[2], words[0]),
    }
    odd_shift = 5 * (row8 & 1)
    by_z_odd = {key: jnp.right_shift(value, odd_shift) for key, value in by_z.items()}

    for ay in range(2):
        slot0 = SLOTS[(ay, 0)]
        own = [ext_ref[slot0, attr, 4:12, :] for attr in range(6)]
        own_six = own[4] * 6.0
        own_twelve = own[5] * 12.0
        total = [jnp.zeros((8, 128), f32) for _ in range(3)]
        for ex, ey, ez in STEPS:
            there = SLOTS[(ay + ey, ez)]
            far = [ext_ref[there, attr, 4 + ex : 12 + ex, :] for attr in range(6)]
            diff = [own[axis] - far[axis] for axis in range(3)]
            dist_sq = diff[0] * diff[0] + diff[1] * diff[1] + diff[2] * diff[2]
            root_inv = lax.rsqrt(dist_sq)
            inverse = root_inv * root_inv
            inverse_six = inverse * inverse * inverse
            dispersion = (own_twelve * far[5] * inverse_six - own_six * far[4]) * inverse_six
            ratio = 1.0 / (1.0 + (0.4 * EWALD_BETA) * (dist_sq * root_inv))
            scaled = jnp.full((8, 128), ERFCX[-1], f32)
            for factor in ERFCX[-2::-1]:
                scaled = scaled * ratio + factor
            gauss = jnp.exp(dist_sq * (-(EWALD_BETA**2)))
            coulomb = own[3] * far[3] * (gauss * (scaled * ratio * root_inv + 2.0 * EWALD_BETA / math.sqrt(math.pi)))
            switch = jnp.maximum(1.0 - dist_sq * (1.0 / (CUTOFF * CUTOFF)), 0.0)
            place = 5 * (ex // 2 + 2) + (ay + ey) // 2 + 2
            word = by_z_odd[ez] if ex % 2 else by_z[ez]
            listed = (word & (1 << place)) != 0
            scalar = jnp.where(listed, (dispersion + coulomb) * inverse * (switch * switch), 0.0)
            for axis in range(3):
                total[axis] = total[axis] + scalar * diff[axis]
        for axis in range(3):
            o_ref[ay, :, axis, :] = total[axis]
    unpack_forces(o_ref, out_ref)


def along(value, axis, step):
    count = lax.axis_size(axis)
    return lax.ppermute(value, axis, [(i, (i + step) % count) for i in range(count)])


def shards(table, particles, pair_list, pair_count):
    big = pltpu.CompilerParams(vmem_limit_bytes=48 * 1024 * 1024)
    packed, send = pl.pallas_call(
        spread_kernel,
        out_shape=(
            jax.ShapeDtypeStruct((4, 8, 8, 128), f32),
            jax.ShapeDtypeStruct((DEVICES, 10, 128), f32),
        ),
        in_specs=[VMEM] * 2,
        out_specs=(VMEM, VMEM),
        scratch_shapes=[pltpu.VMEM((576, 640), f32)],
        compiler_params=big,
    )(particles, table["z"])
    below = along(packed[:, 4:8], "slab", 1)
    above = along(packed[:, 0:4], "slab", -1)
    wide = jnp.concatenate([below, packed, above], axis=1)
    low = along(wide[2], "lane", 1)
    high = along(wide[3], "lane", -1)
    received = lax.all_to_all(send, ("lane", "slab"), split_axis=0, concat_axis=0, tiled=True)
    short_forces = pl.pallas_call(
        near_kernel,
        out_shape=jax.ShapeDtypeStruct((3, 2048), f32),
        in_specs=[VMEM] * 5,
        out_specs=VMEM,
        scratch_shapes=[
            pltpu.VMEM((len(SLOTS), 6, 16, 128), f32),
            pltpu.VMEM((2, 8, 8, 128), f32),
        ],
        compiler_params=big,
    )(wide[0:2], low, high, pair_list, pair_count.reshape(1, 256))
    outgoing = pl.pallas_call(
        middle_kernel,
        out_shape=jax.ShapeDtypeStruct((DEVICES, 10, 128), f32),
        in_specs=[VMEM] * 8,
        out_specs=VMEM,
        scratch_shapes=[pltpu.VMEM((576, 256), f32)],
        compiler_params=big,
    )(received, *(table[name] for name in ("x", "xt", "y", "yt", "col", "row", "plane")))
    returned = lax.all_to_all(outgoing, ("lane", "slab"), split_axis=0, concat_axis=0, tiled=True)
    long_forces = pl.pallas_call(
        force_kernel,
        out_shape=jax.ShapeDtypeStruct((3, 2048), f32),
        in_specs=[VMEM] * 3,
        out_specs=VMEM,
        scratch_shapes=[pltpu.VMEM((576, 640), f32), pltpu.VMEM((2, 8, 8, 128), f32)],
        compiler_params=big,
    )(returned, packed, table["z"])
    return short_forces, long_forces


def solution(mesh):
    table = tables()
    in_specs = (P(None, ("slab", "lane")), P(None, ("slab", "lane")), P(("slab", "lane")))
    out_specs = (P(None, ("slab", "lane")), P(None, ("slab", "lane")))
    body = functools.partial(shards, table)
    return jax.shard_map(body, mesh=mesh, in_specs=in_specs, out_specs=out_specs, check_vma=False)
```
